32 devices in a mesh: tm: 8 (over y, x, core), row: 4 (over z).
Axes of the slice: x: 2, y: 2, z: 4, core: 2. Of those that a mesh axis runs over, the one named last changes fastest.
Arguments:
- feature: bfloat16 [32, 16, 128, 384], P('tm', 'row'), may hold values from -6 to 6
- conv_weight: bfloat16 [3, 3, 3, 384, 384], replicated, may hold values from -0.0625 to 0.0625
- conv_bias: float32 [384], replicated, may hold values from -3 to 3
- down_weight: bfloat16 [3, 2, 2, 384, 16], replicated, may hold values from -0.09375 to 0.09375
- down_bias: float32 [16], replicated, may hold values from -3 to 3
Outputs:
- tokens: float32 [2048, 64], P(('tm', 'row'))
The draws below stay inside these ranges and needn't reach their ends.
All inputs are finite; a program needn't handle non-finite values.
Results may differ from the reference program's by a relative error of at most 0.0022.
Values may be sent and summed in bfloat16 or wider, within the bound.
A program may use at most 128 MiB of HBM per device.

```python
import jax
import jax.numpy as jnp
from jax import lax

C = 384
Z = 16
LW = 64
TLAT = 16
HL = 8
TIN = 32
HIN = 16
WIN = 128
TOKENS = 2048


def shard_levels(own_key, extent, cuts, smallest, top_value):
    gain, own = 1.0, jax.random.fold_in(own_key, 6)
    for dim, parts in cuts:
        steps = jnp.exp(jax.random.uniform(jax.random.fold_in(own, dim), (parts,), jnp.float32, smallest / len(cuts), top_value / len(cuts)))
        gain = gain * jnp.repeat(steps, extent[dim] // parts).reshape([-1 if axis == dim else 1 for axis in range(len(extent))])
    return gain


def gaussian(rng, extent, width, most, split=(), kind=jnp.bfloat16):
    drawn = jax.random.normal(rng, extent, jnp.float32) * width
    if len(split) > 0:
        drawn = shard_levels(rng, extent, split, -0.22, 0.18) * drawn
    return jnp.clip(drawn, min=-most, max=most).astype(kind)


def setup_inputs(seed: int = 0) -> dict:
    arg_keys = jax.random.split(jax.random.key(seed), 6)
    feature = gaussian(arg_keys[0], (TIN, HIN, WIN, C), 1.0, 6.0, ((0, 8), (1, 4)))
    conv_weight = gaussian(arg_keys[1], (3, 3, 3, C, C), (27 * C) ** -0.5, 0.0625)
    conv_bias = gaussian(arg_keys[2], (C,), 0.5, 3.0, (), jnp.float32)
    down_weight = gaussian(arg_keys[3], (3, 2, 2, C, Z), (12 * C) ** -0.5, 0.09375)
    down_bias = gaussian(arg_keys[4], (Z,), 0.5, 3.0, (), jnp.float32)
    return dict(feature=feature, conv_weight=conv_weight, conv_bias=conv_bias, down_weight=down_weight, down_bias=down_bias)


def reference(feature, conv_weight, conv_bias, down_weight, down_bias):
    channels = feature.shape[-1]
    padded = jnp.pad(feature, ((2, 0), (1, 1), (1, 1), (0, 0)))
    kernel = conv_weight.astype(jnp.float32).reshape(27 * channels, channels)

    def one_frame(frame):
        window = lax.dynamic_slice_in_dim(padded, frame, 3, 0)
        pieces = []
        for tap_time in range(3):
            for tap_row in range(3):
                for tap_col in range(3):
                    pieces.append(window[tap_time, tap_row:tap_row + HIN, tap_col:tap_col + WIN, :])
        columns = jnp.concatenate(pieces, axis=-1).astype(jnp.float32).reshape(HIN * WIN, 27 * channels)
        pre = jnp.dot(columns, kernel, precision=lax.Precision.HIGHEST) + conv_bias
        return jax.nn.silu(pre).astype(jnp.bfloat16).reshape(HIN, WIN, channels)

    act = lax.map(one_frame, jnp.arange(TIN, dtype=jnp.int32))
    shifted = jnp.concatenate([jnp.zeros((1, HIN, WIN, channels), jnp.bfloat16), act], axis=0)
    slabs = []
    for tap_time in range(3):
        part = shifted[tap_time:tap_time + 2 * TLAT:2]
        part = part.reshape(TLAT, HL, 2, LW, 2, channels).transpose(0, 1, 3, 2, 4, 5)
        slabs.append(part.reshape(TLAT * HL * LW, 4 * channels))
    stacked = jnp.concatenate(slabs, axis=-1).astype(jnp.float32)
    down = down_weight.astype(jnp.float32).reshape(12 * channels, Z)
    latent = jnp.dot(stacked, down, precision=lax.Precision.HIGHEST) + down_bias
    latent = latent.reshape(TLAT, HL // 2, 2, LW // 2, 2, Z).transpose(0, 1, 3, 2, 4, 5)
    return latent.reshape(TOKENS, 4 * Z)
```

```python
import functools

import jax
import jax.numpy as jnp
from jax import lax
from jax.experimental import pallas as pl
from jax.experimental.pallas import tpu as pltpu
from jax.sharding import PartitionSpec as P

MESH = pl.DeviceIdType.MESH
F32 = jnp.float32
BF16 = jnp.bfloat16


def kernel(
    n_tm, n_row,
    x_ref, cw_ref, cb_ref, dw_ref, db_ref,
    out_ref,
    xs, w, acc, act, wd, s_ref, tx, rx, cx,
    w_sem, x_sem, send_sem, recv_sem, tx_sem, rx_sem, cx_sem,
):
    frames, rows, cols, chans = x_ref.shape
    lat = frames // 2
    tm = lax.axis_index("tm")
    row = lax.axis_index("row")
    up_ok, down_ok = row > 0, row < n_row - 1
    next_ok, prev_ok = tm < n_tm - 1, tm > 0

    last = pl.ds(frames - 2, 2)
    halos = [
        (x_ref.at[:, 0], xs.at[pl.ds(2, frames), rows + 1], 0, -1, up_ok, down_ok),
        (x_ref.at[:, rows - 1], xs.at[pl.ds(2, frames), 0], 0, 1, down_ok, up_ok),
        (x_ref.at[last], xs.at[pl.ds(0, 2), pl.ds(1, rows)], 1, 0, next_ok, prev_ok),
        (x_ref.at[last, 0], xs.at[pl.ds(0, 2), rows + 1], 1, -1, next_ok & up_ok, prev_ok & down_ok),
        (x_ref.at[last, rows - 1], xs.at[pl.ds(0, 2), 0], 1, 1, next_ok & down_ok, prev_ok & up_ok),
    ]

    def halo_copy(k):
        src, dst, dt, dr, _, _ = halos[k]
        return pltpu.make_async_remote_copy(
            src_ref=src, dst_ref=dst, send_sem=send_sem.at[k], recv_sem=recv_sem.at[k],
            device_id={"tm": tm + dt, "row": row + dr}, device_id_type=MESH,
        )

    def owner_of(f):
        unit = f * n_row + row
        return unit // lat, unit % lat

    barrier = pltpu.get_barrier_semaphore()

    def greet(dt, dr, when):
        @pl.when(when)
        def _():
            pl.semaphore_signal(
                barrier, inc=1, device_id={"tm": tm + dt, "row": row + dr}, device_id_type=MESH
            )

    for _, _, dt, dr, _, comes in halos:
        greet(-dt, -dr, comes)
    for slot in range(lat):
        unit = row * lat + slot
        source = unit % n_row
        greet(0, source - row, source != row)
        greet(-1, source - row, prev_ok & (unit < n_row))

    x_copy = pltpu.make_async_copy(x_ref, xs.at[pl.ds(2, frames), pl.ds(1, rows)], x_sem)
    x_copy.start()
    w_copies = []
    for a in range(3):
        for b in range(3):
            for c in range(3):
                w_copies.append(
                    pltpu.make_async_copy(
                        cw_ref.at[a, b, c],
                        w.at[pl.ds((3 * a + b) * chans, chans), pl.ds(c * chans, chans)],
                        w_sem.at[9 * a + 3 * b + c],
                    )
                )
                w_copies[-1].start()

    targets = [goes for _, _, _, _, goes, _ in halos] + [next_ok]
    targets += [owner_of(f)[0] != row for f in range(lat)]
    pl.semaphore_wait(barrier, sum(jnp.where(goes, 1, 0) for goes in targets))

    for k in range(5):
        @pl.when(halos[k][4])
        def _(k=k):
            halo_copy(k).start()

    @pl.when(row == 0)
    def _():
        xs[:, 0] = jnp.zeros((frames + 2, cols, chans), BF16)

    @pl.when(row == n_row - 1)
    def _():
        xs[:, rows + 1] = jnp.zeros((frames + 2, cols, chans), BF16)

    @pl.when(tm == 0)
    def _():
        xs[0:2] = jnp.zeros((2, rows + 2, cols, chans), BF16)

    zi = lax.broadcasted_iota(jnp.int32, (16, 128), 0)
    li = lax.broadcasted_iota(jnp.int32, (16, 128), 1)
    spread = [((li % 16 == zi) & (li // 64 == dx)).astype(F32).astype(BF16) for dx in range(2)]
    for a in range(3):
        for dy in range(2):
            part = sum(
                lax.dot_general(
                    dw_ref[a, dy, dx], spread[dx], (((0,), (0,)), ((), ())),
                    preferred_element_type=F32,
                )
                for dx in range(2)
            )
            wd[a * chans : (a + 1) * chans, dy * 128 : (dy + 1) * 128] = part.astype(BF16)

    x_copy.wait()
    for copy in w_copies:
        copy.wait()

    pairs = frames // 2
    early = pairs - 1
    row_id = lax.broadcasted_iota(jnp.int32, (cols, chans), 0)

    def await_halo(k, when):
        @pl.when(when & halos[k][5])
        def _():
            halo_copy(k).wait_recv()

    def conv_step(step, _):
        await_halo(0, step == early)
        await_halo(1, step == early)
        await_halo(2, step == 2 * early)
        await_halo(3, step == 2 * early + 1)
        await_halo(4, step == 2 * early + 1)
        is_late = step >= 2 * early
        outer = jnp.where(is_late, step - 2 * early, (step >= early).astype(jnp.int32))
        pair = jnp.where(is_late, 0, step - outer * early + 1)
        first = 2 * pair
        places = [(df, i) for df in range(2) for i in range(2)]
        spots = [(first + df, 1 - outer if i == 0 else 2 + outer) for df, i in places]
        pieces = []
        for a in range(3):
            for b in range(3):
                pieces.append(jnp.concatenate([xs[f + a, i + b] for f, i in spots], axis=0))
        lhs = jnp.concatenate(pieces, axis=1)
        acc[:, : 2 * chans] = jnp.dot(lhs, w[:, : 2 * chans], preferred_element_type=F32)
        acc[:, 2 * chans :] = jnp.dot(lhs, w[:, 2 * chans :], preferred_element_type=F32)
        for n, (f, i) in enumerate(spots):
            span = slice(n * cols, (n + 1) * cols)
            left = pltpu.roll(acc[span, :chans], 1, 0)
            right = pltpu.roll(acc[span, 2 * chans :], cols - 1, 0)
            pre = acc[span, chans : 2 * chans] + cb_ref[...]
            pre += jnp.where(row_id == 0, 0.0, left)
            pre += jnp.where(row_id == cols - 1, 0.0, right)
            act[f, i] = (pre / (1.0 + jnp.exp(-pre))).astype(BF16)
        return 0

    lax.fori_loop(0, 2 * pairs, conv_step, 0)

    lane = lax.broadcasted_iota(jnp.int32, (cols // 4, 128), 1)

    def project(parts):
        lhs = jnp.concatenate([act[f].reshape(rows * cols, chans) for f, _ in parts], axis=1)
        low = parts[0][1] * chans
        weights = wd[low : low + len(parts) * chans]
        both = jnp.dot(lhs, weights, preferred_element_type=F32)
        s_ref[0] = both[:, :128]
        s_ref[1] = both[:, 128:]
        even = jnp.zeros((cols // 4, 128), F32)
        odd = jnp.zeros((cols // 4, 128), F32)
        for block in range(4):
            dyo, dxo = block // 2, block % 2
            sums = []
            for dx in range(2):
                sums.append(sum(
                    s_ref[dy, pl.ds((2 * dyo + dy) * cols + 2 * dxo + dx, cols // 4, stride=4), :]
                    for dy in range(2)
                ))
            even = jnp.where(lane // 16 == block, sums[0], even)
            odd = jnp.where(lane // 16 == block + 4, sums[1], odd)
        return even + pltpu.roll(odd, 64, 1)

    def unit_copy(f):
        owner, slot = owner_of(f)
        return pltpu.make_async_remote_copy(
            src_ref=tx.at[f], dst_ref=rx.at[slot], send_sem=tx_sem.at[f], recv_sem=rx_sem.at[slot],
            device_id={"tm": tm, "row": owner}, device_id_type=MESH,
        )

    def tail_copy():
        owner, slot = owner_of(0)
        return pltpu.make_async_remote_copy(
            src_ref=tx.at[lat], dst_ref=cx.at[slot], send_sem=tx_sem.at[lat],
            recv_sem=cx_sem.at[slot],
            device_id={"tm": tm + 1, "row": owner}, device_id_type=MESH,
        )

    tx[lat] = project([(frames - 1, 0)])

    @pl.when(next_ok)
    def _():
        tail_copy().start()

    for f in range(lat):
        if f == 0:
            tokens = project([(0, 1), (1, 2)])
        else:
            tokens = project([(2 * f - 1, 0), (2 * f, 1), (2 * f + 1, 2)])
        owner, slot = owner_of(f)
        tx[f] = tokens

        @pl.when(owner == row)
        def _():
            rx[slot] = tokens

        @pl.when(owner != row)
        def _():
            unit_copy(f).start()

    bias = jnp.concatenate([db_ref[...]] * 4, axis=1)
    quarter = cols // 4
    for slot in range(lat):
        unit = row * lat + slot

        @pl.when(unit % n_row != row)
        def _():
            pltpu.make_async_remote_copy(
                src_ref=tx.at[0], dst_ref=rx.at[slot], send_sem=tx_sem.at[0],
                recv_sem=rx_sem.at[slot],
                device_id={"tm": tm, "row": unit % n_row}, device_id_type=MESH,
            ).wait_recv()

        out_ref[slot * quarter : (slot + 1) * quarter, :] = rx[slot][:, :64] + bias

        @pl.when(prev_ok & (unit < n_row))
        def _():
            pltpu.make_async_remote_copy(
                src_ref=tx.at[lat], dst_ref=cx.at[slot], send_sem=tx_sem.at[lat],
                recv_sem=cx_sem.at[slot],
                device_id={"tm": tm - 1, "row": unit % n_row}, device_id_type=MESH,
            ).wait_recv()
            out_ref[slot * quarter : (slot + 1) * quarter, :] += cx[slot][:, :64]

    for k in range(5):
        @pl.when(halos[k][4])
        def _(k=k):
            halo_copy(k).wait_send()

    @pl.when(next_ok)
    def _():
        tail_copy().wait_send()

    for f in range(lat):
        @pl.when(owner_of(f)[0] != row)
        def _(f=f):
            unit_copy(f).wait_send()


def on_device(n_tm, n_row, feature, conv_weight, conv_bias, down_weight, down_bias):
    frames, rows, cols, chans = feature.shape
    lat = frames // 2
    vmem = pl.BlockSpec(memory_space=pltpu.VMEM)
    anywhere = pl.BlockSpec(memory_space=pl.ANY)
    flops = 2 * frames * rows * cols * 27 * chans * chans
    return pl.pallas_call(
        functools.partial(kernel, n_tm, n_row),
        out_shape=jax.ShapeDtypeStruct((lat * cols // 4, 64), F32),
        in_specs=[anywhere, anywhere, vmem, vmem, vmem],
        out_specs=vmem,
        scratch_shapes=[
            pltpu.VMEM((frames + 2, rows + 2, cols, chans), BF16),
            pltpu.VMEM((9 * chans, 3 * chans), BF16),
            pltpu.VMEM((4 * cols, 3 * chans), F32),
            pltpu.VMEM((frames, rows, cols, chans), BF16),
            pltpu.VMEM((3 * chans, 256), BF16),
            pltpu.VMEM((2, rows * cols, 128), F32),
            pltpu.VMEM((lat + 1, cols // 4, 128), F32),
            pltpu.VMEM((lat, cols // 4, 128), F32),
            pltpu.VMEM((lat, cols // 4, 128), F32),
            pltpu.SemaphoreType.DMA((27,)),
            pltpu.SemaphoreType.DMA,
            pltpu.SemaphoreType.DMA((5,)),
            pltpu.SemaphoreType.DMA((5,)),
            pltpu.SemaphoreType.DMA((lat + 1,)),
            pltpu.SemaphoreType.DMA((lat,)),
            pltpu.SemaphoreType.DMA((lat,)),
        ],
        compiler_params=pltpu.CompilerParams(
            collective_id=0, has_side_effects=True, vmem_limit_bytes=56 * 1024 * 1024
        ),
        cost_estimate=pl.CostEstimate(flops=flops, bytes_accessed=12 << 20, transcendentals=0),
    )(feature, conv_weight, conv_bias.reshape(1, -1), down_weight.swapaxes(3, 4), down_bias.reshape(1, -1))


def solution(mesh):
    return jax.shard_map(
        functools.partial(on_device, mesh.shape["tm"], mesh.shape["row"]),
        mesh=mesh,
        in_specs=(P("tm", "row", None, None), P(), P(), P(), P()),
        out_specs=P(("tm", "row"), None),
        check_vma=False,
    )
```

```python
import functools

import jax
import jax.numpy as jnp
from jax import lax
from jax.experimental import pallas as pl
from jax.experimental.pallas import tpu as pltpu
from jax.sharding import PartitionSpec as P

MESH = pl.DeviceIdType.MESH
F32 = jnp.float32
BF16 = jnp.bfloat16


def kernel(
    n_tm, n_row,
    x_ref, cw_ref, cb_ref, dw_ref, db_ref,
    out_ref,
    xs, w, acc_a, acc_b, hold, act, wd, s_ref, tx, rx, cx,
    w_sem, x_sem, send_sem, recv_sem, tx_sem, rx_sem, cx_sem,
):
    frames, rows, cols, chans = x_ref.shape
    lat = frames // 2
    tm = lax.axis_index("tm")
    row = lax.axis_index("row")
    up_ok, down_ok = row > 0, row < n_row - 1
    next_ok, prev_ok = tm < n_tm - 1, tm > 0

    last = pl.ds(frames - 2, 2)
    halos = [
        (x_ref.at[:, 0], xs.at[pl.ds(2, frames), rows + 1], 0, -1, up_ok, down_ok),
        (x_ref.at[:, rows - 1], xs.at[pl.ds(2, frames), 0], 0, 1, down_ok, up_ok),
        (x_ref.at[last], xs.at[pl.ds(0, 2), pl.ds(1, rows)], 1, 0, next_ok, prev_ok),
        (x_ref.at[last, 0], xs.at[pl.ds(0, 2), rows + 1], 1, -1, next_ok & up_ok, prev_ok & down_ok),
        (x_ref.at[last, rows - 1], xs.at[pl.ds(0, 2), 0], 1, 1, next_ok & down_ok, prev_ok & up_ok),
    ]

    def halo_copy(k):
        src, dst, dt, dr, _, _ = halos[k]
        return pltpu.make_async_remote_copy(
            src_ref=src, dst_ref=dst, send_sem=send_sem.at[k], recv_sem=recv_sem.at[k],
            device_id={"tm": tm + dt, "row": row + dr}, device_id_type=MESH,
        )

    def owner_of(f):
        unit = f * n_row + row
        return unit // lat, unit % lat

    barrier = pltpu.get_barrier_semaphore()

    def greet(dt, dr, when):
        @pl.when(when)
        def _():
            pl.semaphore_signal(
                barrier, inc=1, device_id={"tm": tm + dt, "row": row + dr}, device_id_type=MESH
            )

    for _, _, dt, dr, _, comes in halos:
        greet(-dt, -dr, comes)
    for slot in range(lat):
        unit = row * lat + slot
        source = unit % n_row
        greet(0, source - row, source != row)
        greet(-1, source - row, prev_ok & (unit < n_row))

    x_copy = pltpu.make_async_copy(x_ref, xs.at[pl.ds(2, frames), pl.ds(1, rows)], x_sem)
    x_copy.start()
    w_copies = []
    for a in range(3):
        for b in range(3):
            for c in range(3):
                w_copies.append(
                    pltpu.make_async_copy(
                        cw_ref.at[a, b, c],
                        w.at[pl.ds((3 * a + b) * chans, chans), pl.ds(c * chans, chans)],
                        w_sem.at[9 * a + 3 * b + c],
                    )
                )

    for copy in w_copies[18:] + w_copies[:18]:
        copy.start()

    targets = [goes for _, _, _, _, goes, _ in halos] + [next_ok]
    targets += [owner_of(f)[0] != row for f in range(lat)]
    pl.semaphore_wait(barrier, sum(jnp.where(goes, 1, 0) for goes in targets))

    for k in range(3):
        @pl.when(halos[k][4])
        def _(k=k):
            halo_copy(k).start()

    @pl.when(row == 0)
    def _():
        xs[:, 0] = jnp.zeros((frames + 2, cols, chans), BF16)

    @pl.when(row == n_row - 1)
    def _():
        xs[:, rows + 1] = jnp.zeros((frames + 2, cols, chans), BF16)

    @pl.when(tm == 0)
    def _():
        xs[0:2] = jnp.zeros((2, rows + 2, cols, chans), BF16)

    zi = lax.broadcasted_iota(jnp.int32, (16, 128), 0)
    li = lax.broadcasted_iota(jnp.int32, (16, 128), 1)
    spread = [((li % 16 == zi) & (li // 64 == dx)).astype(F32).astype(BF16) for dx in range(2)]
    for a in range(3):
        for dy in range(2):
            part = sum(
                lax.dot_general(
                    dw_ref[a, dy, dx], spread[dx], (((0,), (0,)), ((), ())),
                    preferred_element_type=F32,
                )
                for dx in range(2)
            )
            wd[a * chans : (a + 1) * chans, dy * 128 : (dy + 1) * 128] = part.astype(BF16)

    x_copy.wait()

    pairs = frames // 2
    row_id = lax.broadcasted_iota(jnp.int32, (cols, chans), 0)
    bias_row = cb_ref[...].reshape(1, chans)

    def await_halo(k):
        @pl.when(halos[k][5])
        def _():
            halo_copy(k).wait_recv()

    def spots_of(pair, outer):
        picked = (0, rows - 1) if outer else (1, rows - 2)
        return [(2 * pair + df, i) for df in range(2) for i in picked]

    def gathered(spots, taps):
        pieces = []
        for a in taps:
            for b in range(3):
                pieces.append(jnp.concatenate([xs[f + a, i + b] for f, i in spots], axis=0))
        return jnp.concatenate(pieces, axis=1)

    def multiply(into, spots, taps, plus=None):
        lhs = gathered(spots, taps)
        span = slice(taps[0] * 3 * chans, (taps[-1] + 1) * 3 * chans)
        for lanes in (slice(0, 2 * chans), slice(2 * chans, 3 * chans)):
            part = jnp.dot(lhs, w[span, lanes], preferred_element_type=F32)
            into[:, lanes] = part if plus is None else part + plus[:, lanes]

    def activate(source, spots):
        for n, (f, i) in enumerate(spots):
            span = slice(n * cols, (n + 1) * cols)
            left = pltpu.roll(source[span, :chans], 1, 0)
            right = pltpu.roll(source[span, 2 * chans :], cols - 1, 0)
            pre = source[span, chans : 2 * chans] + bias_row
            pre += jnp.where(row_id == 0, 0.0, left)
            pre += jnp.where(row_id == cols - 1, 0.0, right)
            half = 0.5 * pre
            act[f, i] = (half + half * jnp.tanh(half)).astype(BF16)

    for copy in w_copies[18:]:
        copy.wait()
    multiply(hold, spots_of(0, False), (2,))
    for copy in w_copies[:18]:
        copy.wait()
    sums = [acc_a, acc_b]
    done = []

    def block(pair, outer, taps=(0, 1, 2), plus=None):
        spots = spots_of(pair, outer)
        into = sums[len(done) % 2]
        multiply(into, spots, taps, plus)
        if done:
            activate(*done[-1])
        done.append((into, spots))

    for pair in range(1, pairs):
        block(pair, False)
    for k in (3, 4):
        @pl.when(halos[k][4])
        def _(k=k):
            halo_copy(k).start()
    for k in (0, 1):
        await_halo(k)
    for pair in range(1, pairs):
        block(pair, True)
    await_halo(2)
    block(0, False, (0, 1), hold)
    for k in (3, 4):
        await_halo(k)

    lane = lax.broadcasted_iota(jnp.int32, (cols // 4, 128), 1)

    def project(parts):
        lhs = jnp.concatenate([act[f].reshape(rows * cols, chans) for f, _ in parts], axis=1)
        low = parts[0][1] * chans
        weights = wd[low : low + len(parts) * chans]
        both = jnp.dot(lhs, weights, preferred_element_type=F32)
        s_ref[0] = both[:, :128]
        s_ref[1] = both[:, 128:]
        even = jnp.zeros((cols // 4, 128), F32)
        odd = jnp.zeros((cols // 4, 128), F32)
        for block in range(4):
            dyo, dxo = block // 2, block % 2
            sums = []
            for dx in range(2):
                sums.append(sum(
                    s_ref[dy, pl.ds((2 * dyo + dy) * cols + 2 * dxo + dx, cols // 4, stride=4), :]
                    for dy in range(2)
                ))
            even = jnp.where(lane // 16 == block, sums[0], even)
            odd = jnp.where(lane // 16 == block + 4, sums[1], odd)
        return even + pltpu.roll(odd, 64, 1)

    def unit_copy(f):
        owner, slot = owner_of(f)
        return pltpu.make_async_remote_copy(
            src_ref=tx.at[f], dst_ref=rx.at[slot], send_sem=tx_sem.at[f], recv_sem=rx_sem.at[slot],
            device_id={"tm": tm, "row": owner}, device_id_type=MESH,
        )

    def tail_copy():
        owner, slot = owner_of(0)
        return pltpu.make_async_remote_copy(
            src_ref=tx.at[lat], dst_ref=cx.at[slot], send_sem=tx_sem.at[lat],
            recv_sem=cx_sem.at[slot],
            device_id={"tm": tm + 1, "row": owner}, device_id_type=MESH,
        )

    tx[lat] = project([(frames - 1, 0)])
    block(0, True)

    @pl.when(next_ok)
    def _():
        tail_copy().start()

    activate(*done[-1])
    for f in reversed(range(lat)):
        if f == 0:
            tokens = project([(0, 1), (1, 2)])
        else:
            tokens = project([(2 * f - 1, 0), (2 * f, 1), (2 * f + 1, 2)])
        owner, slot = owner_of(f)
        tx[f] = tokens

        @pl.when(owner == row)
        def _():
            rx[slot] = tokens

        @pl.when(owner != row)
        def _():
            unit_copy(f).start()

    bias = jnp.concatenate([db_ref[...]] * 4, axis=1)
    quarter = cols // 4
    for slot in range(lat):
        unit = row * lat + slot

        @pl.when(unit % n_row != row)
        def _():
            pltpu.make_async_remote_copy(
                src_ref=tx.at[0], dst_ref=rx.at[slot], send_sem=tx_sem.at[0],
                recv_sem=rx_sem.at[slot],
                device_id={"tm": tm, "row": unit % n_row}, device_id_type=MESH,
            ).wait_recv()

        out_ref[slot * quarter : (slot + 1) * quarter, :] = rx[slot][:, :64] + bias

        @pl.when(prev_ok & (unit < n_row))
        def _():
            pltpu.make_async_remote_copy(
                src_ref=tx.at[lat], dst_ref=cx.at[slot], send_sem=tx_sem.at[lat],
                recv_sem=cx_sem.at[slot],
                device_id={"tm": tm - 1, "row": unit % n_row}, device_id_type=MESH,
            ).wait_recv()
            out_ref[slot * quarter : (slot + 1) * quarter, :] += cx[slot][:, :64]

    for k in range(5):
        @pl.when(halos[k][4])
        def _(k=k):
            halo_copy(k).wait_send()

    @pl.when(next_ok)
    def _():
        tail_copy().wait_send()

    for f in range(lat):
        @pl.when(owner_of(f)[0] != row)
        def _(f=f):
            unit_copy(f).wait_send()


def on_device(n_tm, n_row, feature, conv_weight, conv_bias, down_weight, down_bias):
    frames, rows, cols, chans = feature.shape
    lat = frames // 2
    vmem = pl.BlockSpec(memory_space=pltpu.VMEM)
    anywhere = pl.BlockSpec(memory_space=pl.ANY)
    flops = 2 * frames * rows * cols * 27 * chans * chans
    return pl.pallas_call(
        functools.partial(kernel, n_tm, n_row),
        out_shape=jax.ShapeDtypeStruct((lat * cols // 4, 64), F32),
        in_specs=[anywhere, anywhere, vmem, vmem, vmem],
        out_specs=vmem,
        scratch_shapes=[
            pltpu.VMEM((frames + 2, rows + 2, cols, chans), BF16),
            pltpu.VMEM((9 * chans, 3 * chans), BF16),
            pltpu.VMEM((4 * cols, 3 * chans), F32),
            pltpu.VMEM((4 * cols, 3 * chans), F32),
            pltpu.VMEM((4 * cols, 3 * chans), F32),
            pltpu.VMEM((frames, rows, cols, chans), BF16),
            pltpu.VMEM((3 * chans, 256), BF16),
            pltpu.VMEM((2, rows * cols, 128), F32),
            pltpu.VMEM((lat + 1, cols // 4, 128), F32),
            pltpu.VMEM((lat, cols // 4, 128), F32),
            pltpu.VMEM((lat, cols // 4, 128), F32),
            pltpu.SemaphoreType.DMA((27,)),
            pltpu.SemaphoreType.DMA,
            pltpu.SemaphoreType.DMA((5,)),
            pltpu.SemaphoreType.DMA((5,)),
            pltpu.SemaphoreType.DMA((lat + 1,)),
            pltpu.SemaphoreType.DMA((lat,)),
            pltpu.SemaphoreType.DMA((lat,)),
        ],
        compiler_params=pltpu.CompilerParams(
            collective_id=0, has_side_effects=True, vmem_limit_bytes=56 * 1024 * 1024
        ),
        cost_estimate=pl.CostEstimate(flops=flops, bytes_accessed=12 << 20, transcendentals=0),
    )(feature, conv_weight, conv_bias, down_weight.swapaxes(3, 4), down_bias.reshape(1, -1))


def solution(mesh):
    return jax.shard_map(
        functools.partial(on_device, mesh.shape["tm"], mesh.shape["row"]),
        mesh=mesh,
        in_specs=(P("tm", "row", None, None), P(), P(), P(), P()),
        out_specs=P(("tm", "row"), None),
        check_vma=False,
    )
```

```python
import functools

import jax
import jax.numpy as jnp
from jax import lax
from jax.experimental import pallas as pl
from jax.experimental.pallas import tpu as pltpu
from jax.sharding import PartitionSpec as P

MESH = pl.DeviceIdType.MESH
F32 = jnp.float32
BF16 = jnp.bfloat16


def kernel(
    n_tm, n_row,
    x_ref, cw_ref, cb_ref, dw_ref, db_ref,
    out_ref,
    xs, w, acc, act, wd, s_ref, tx, rx, cx,
    w_sem, x_sem, send_sem, recv_sem, tx_sem, rx_sem, cx_sem,
):
    frames, rows, cols, chans = x_ref.shape
    lat = frames // 2
    tm = lax.axis_index("tm")
    row = lax.axis_index("row")
    up_ok, down_ok = row > 0, row < n_row - 1
    next_ok, prev_ok = tm < n_tm - 1, tm > 0

    last = pl.ds(frames - 2, 2)
    halos = [
        (x_ref.at[:, 0], xs.at[pl.ds(2, frames), rows + 1], 0, -1, up_ok, down_ok),
        (x_ref.at[:, rows - 1], xs.at[pl.ds(2, frames), 0], 0, 1, down_ok, up_ok),
        (x_ref.at[last], xs.at[pl.ds(0, 2), pl.ds(1, rows)], 1, 0, next_ok, prev_ok),
        (x_ref.at[last, 0], xs.at[pl.ds(0, 2), rows + 1], 1, -1, next_ok & up_ok, prev_ok & down_ok),
        (x_ref.at[last, rows - 1], xs.at[pl.ds(0, 2), 0], 1, 1, next_ok & down_ok, prev_ok & up_ok),
    ]

    def halo_copy(k):
        src, dst, dt, dr, _, _ = halos[k]
        return pltpu.make_async_remote_copy(
            src_ref=src, dst_ref=dst, send_sem=send_sem.at[k], recv_sem=recv_sem.at[k],
            device_id={"tm": tm + dt, "row": row + dr}, device_id_type=MESH,
        )

    def owner_of(f):
        unit = f * n_row + row
        return unit // lat, unit % lat

    barrier = pltpu.get_barrier_semaphore()

    def greet(dt, dr, when):
        @pl.when(when)
        def _():
            pl.semaphore_signal(
                barrier, inc=1, device_id={"tm": tm + dt, "row": row + dr}, device_id_type=MESH
            )

    for _, _, dt, dr, _, comes in halos:
        greet(-dt, -dr, comes)
    for slot in range(lat):
        unit = row * lat + slot
        source = unit % n_row
        greet(0, source - row, source != row)
        greet(-1, source - row, prev_ok & (unit < n_row))

    x_copy = pltpu.make_async_copy(x_ref, xs.at[pl.ds(2, frames), pl.ds(1, rows)], x_sem)
    x_copy.start()
    w_copies = []
    for a in range(3):
        for b in range(3):
            for c in range(3):
                w_copies.append(
                    pltpu.make_async_copy(
                        cw_ref.at[a, b, c],
                        w.at[a, pl.ds(b * chans, chans), pl.ds(c * chans, chans)],
                        w_sem.at[9 * a + 3 * b + c],
                    )
                )

    for copy in w_copies[18:] + w_copies[:18]:
        copy.start()

    bias_row = jnp.broadcast_to(cb_ref[...].reshape(1, chans), (4 * cols, chans))
    for n in range(frames):
        acc[n, :, :chans] = jnp.zeros((4 * cols, chans), F32)
        acc[n, :, chans : 2 * chans] = bias_row
        acc[n, :, 2 * chans :] = jnp.zeros((4 * cols, chans), F32)

    targets = [goes for _, _, _, _, goes, _ in halos] + [next_ok]
    targets += [owner_of(f)[0] != row for f in range(lat)]
    pl.semaphore_wait(barrier, sum(jnp.where(goes, 1, 0) for goes in targets))

    for k in range(3):
        @pl.when(halos[k][4])
        def _(k=k):
            halo_copy(k).start()

    @pl.when(row == 0)
    def _():
        xs[:, 0] = jnp.zeros((frames + 2, cols, chans), BF16)

    @pl.when(row == n_row - 1)
    def _():
        xs[:, rows + 1] = jnp.zeros((frames + 2, cols, chans), BF16)

    @pl.when(tm == 0)
    def _():
        xs[0:2] = jnp.zeros((2, rows + 2, cols, chans), BF16)

    zi = lax.broadcasted_iota(jnp.int32, (16, 128), 0)
    li = lax.broadcasted_iota(jnp.int32, (16, 128), 1)
    spread = [((li % 16 == zi) & (li // 64 == dx)).astype(F32).astype(BF16) for dx in range(2)]
    for a in range(3):
        for dy in range(2):
            part = sum(
                lax.dot_general(
                    dw_ref[a, dy, dx], spread[dx], (((0,), (0,)), ((), ())),
                    preferred_element_type=F32,
                )
                for dx in range(2)
            )
            wd[a * chans : (a + 1) * chans, dy * 128 : (dy + 1) * 128] = part.astype(BF16)

    x_copy.wait()

    pairs = frames // 2
    row_id = lax.broadcasted_iota(jnp.int32, (cols, chans), 0)

    def activate(source, spots):
        for n, (f, i) in enumerate(spots):
            span = slice(n * cols, (n + 1) * cols)
            left = pltpu.roll(source[span, :chans], 1, 0)
            right = pltpu.roll(source[span, 2 * chans :], cols - 1, 0)
            pre = source[span, chans : 2 * chans]
            pre += jnp.where(row_id == 0, 0.0, left)
            pre += jnp.where(row_id == cols - 1, 0.0, right)
            half = 0.5 * pre
            act[f, i] = (half + half * jnp.tanh(half)).astype(BF16)

    lane = lax.broadcasted_iota(jnp.int32, (cols // 4, 128), 1)

    def project(parts):
        lhs = jnp.concatenate([act[f].reshape(rows * cols, chans) for f, _ in parts], axis=1)
        low = parts[0][1] * chans
        weights = wd[low : low + len(parts) * chans]
        both = jnp.dot(lhs, weights, preferred_element_type=F32)
        s_ref[0] = both[:, :128]
        s_ref[1] = both[:, 128:]
        even = jnp.zeros((cols // 4, 128), F32)
        odd = jnp.zeros((cols // 4, 128), F32)
        for block in range(4):
            dyo, dxo = block // 2, block % 2
            sums = []
            for dx in range(2):
                sums.append(sum(
                    s_ref[dy, pl.ds((2 * dyo + dy) * cols + 2 * dxo + dx, cols // 4, stride=4), :]
                    for dy in range(2)
                ))
            even = jnp.where(lane // 16 == block, sums[0], even)
            odd = jnp.where(lane // 16 == block + 4, sums[1], odd)
        return even + pltpu.roll(odd, 64, 1)

    def unit_copy(f):
        owner, slot = owner_of(f)
        return pltpu.make_async_remote_copy(
            src_ref=tx.at[f], dst_ref=rx.at[slot], send_sem=tx_sem.at[f], recv_sem=rx_sem.at[slot],
            device_id={"tm": tm, "row": owner}, device_id_type=MESH,
        )

    def tail_copy():
        owner, slot = owner_of(0)
        return pltpu.make_async_remote_copy(
            src_ref=tx.at[lat], dst_ref=cx.at[slot], send_sem=tx_sem.at[lat],
            recv_sem=cx_sem.at[slot],
            device_id={"tm": tm + 1, "row": owner}, device_id_type=MESH,
        )

    early = 3 * (pairs - 1)
    begin_late = 1 + 2 * early

    def conv_step(step, _):
        @pl.when(step == 0)
        def _():
            for copy in w_copies[18:]:
                copy.wait()

        @pl.when(step == 2)
        def _():
            for copy in w_copies[:9]:
                copy.wait()

        @pl.when(step == 3)
        def _():
            for copy in w_copies[9:18]:
                copy.wait()

        @pl.when(step == 1 + early)
        def _():
            for k in (3, 4):
                @pl.when(halos[k][4])
                def _(k=k):
                    halo_copy(k).start()

        for k, at in enumerate((1 + early, 1 + early, begin_late + 1, begin_late + 3, begin_late + 3)):
            @pl.when((step == at) & halos[k][5])
            def _(k=k):
                halo_copy(k).wait_recv()

        late = step - begin_late
        is_late = late >= 0
        is_first = step == 0
        outer = jnp.where(
            is_late, jnp.where((late == 0) | (late > 2), 1, 0), jnp.where(step > early, 1, 0)
        )
        turn = jnp.maximum(step - 1 - jnp.where(step > early, early, 0), 0)
        pair = jnp.where(is_late | is_first, 0, 1 + turn // 3)
        tap = jnp.where(
            is_late,
            jnp.where(late == 0, 2, jnp.where(late > 2, late - 3, late - 1)),
            jnp.where(is_first, 2, (turn + 2) % 3),
        )
        spots = [(2 * pair + df, i) for df in range(2) for i in (1 - outer, rows - 2 + outer)]
        lhs = jnp.concatenate(
            [jnp.concatenate([xs[f + tap, i + b] for f, i in spots], axis=0) for b in range(3)],
            axis=1,
        )
        into = acc.at[2 * pair + outer]
        for lanes in (slice(0, 2 * chans), slice(2 * chans, 3 * chans)):
            into[:, lanes] += jnp.dot(lhs, w[tap, :, lanes], preferred_element_type=F32)

        @pl.when(tap == 1)
        def _():
            activate(into, spots)

        @pl.when(step == begin_late)
        def _():
            tx[lat] = project([(frames - 1, 0)])

            @pl.when(next_ok)
            def _():
                tail_copy().start()

        return 0

    lax.fori_loop(0, 6 * pairs, conv_step, 0)

    for f in reversed(range(lat)):
        if f == 0:
            tokens = project([(0, 1), (1, 2)])
        else:
            tokens = project([(2 * f - 1, 0), (2 * f, 1), (2 * f + 1, 2)])
        owner, slot = owner_of(f)
        tx[f] = tokens

        @pl.when(owner == row)
        def _():
            rx[slot] = tokens

        @pl.when(owner != row)
        def _():
            unit_copy(f).start()

    bias = jnp.concatenate([db_ref[...]] * 4, axis=1)
    quarter = cols // 4
    for slot in range(lat):
        unit = row * lat + slot

        @pl.when(unit % n_row != row)
        def _():
            pltpu.make_async_remote_copy(
                src_ref=tx.at[0], dst_ref=rx.at[slot], send_sem=tx_sem.at[0],
                recv_sem=rx_sem.at[slot],
                device_id={"tm": tm, "row": unit % n_row}, device_id_type=MESH,
            ).wait_recv()

        out_ref[slot * quarter : (slot + 1) * quarter, :] = rx[slot][:, :64] + bias

        @pl.when(prev_ok & (unit < n_row))
        def _():
            pltpu.make_async_remote_copy(
                src_ref=tx.at[lat], dst_ref=cx.at[slot], send_sem=tx_sem.at[lat],
                recv_sem=cx_sem.at[slot],
                device_id={"tm": tm - 1, "row": unit % n_row}, device_id_type=MESH,
            ).wait_recv()
            out_ref[slot * quarter : (slot + 1) * quarter, :] += cx[slot][:, :64]

    for k in range(5):
        @pl.when(halos[k][4])
        def _(k=k):
            halo_copy(k).wait_send()

    @pl.when(next_ok)
    def _():
        tail_copy().wait_send()

    for f in range(lat):
        @pl.when(owner_of(f)[0] != row)
        def _(f=f):
            unit_copy(f).wait_send()


def on_device(n_tm, n_row, feature, conv_weight, conv_bias, down_weight, down_bias):
    frames, rows, cols, chans = feature.shape
    lat = frames // 2
    vmem = pl.BlockSpec(memory_space=pltpu.VMEM)
    anywhere = pl.BlockSpec(memory_space=pl.ANY)
    flops = 2 * frames * rows * cols * 27 * chans * chans
    return pl.pallas_call(
        functools.partial(kernel, n_tm, n_row),
        out_shape=jax.ShapeDtypeStruct((lat * cols // 4, 64), F32),
        in_specs=[anywhere, anywhere, vmem, vmem, vmem],
        out_specs=vmem,
        scratch_shapes=[
            pltpu.VMEM((frames + 2, rows + 2, cols, chans), BF16),
            pltpu.VMEM((3, 3 * chans, 3 * chans), BF16),
            pltpu.VMEM((frames, 4 * cols, 3 * chans), F32),
            pltpu.VMEM((frames, rows, cols, chans), BF16),
            pltpu.VMEM((3 * chans, 256), BF16),
            pltpu.VMEM((2, rows * cols, 128), F32),
            pltpu.VMEM((lat + 1, cols // 4, 128), F32),
            pltpu.VMEM((lat, cols // 4, 128), F32),
            pltpu.VMEM((lat, cols // 4, 128), F32),
            pltpu.SemaphoreType.DMA((27,)),
            pltpu.SemaphoreType.DMA,
            pltpu.SemaphoreType.DMA((5,)),
            pltpu.SemaphoreType.DMA((5,)),
            pltpu.SemaphoreType.DMA((lat + 1,)),
            pltpu.SemaphoreType.DMA((lat,)),
            pltpu.SemaphoreType.DMA((lat,)),
        ],
        compiler_params=pltpu.CompilerParams(
            collective_id=0, has_side_effects=True, vmem_limit_bytes=56 * 1024 * 1024
        ),
        cost_estimate=pl.CostEstimate(flops=flops, bytes_accessed=12 << 20, transcendentals=0),
    )(feature, conv_weight, conv_bias, down_weight.swapaxes(3, 4), down_bias.reshape(1, -1))


def solution(mesh):
    return jax.shard_map(
        functools.partial(on_device, mesh.shape["tm"], mesh.shape["row"]),
        mesh=mesh,
        in_specs=(P("tm", "row", None, None), P(), P(), P(), P()),
        out_specs=P(("tm", "row"), None),
        check_vma=False,
    )
```
